512 devices in a mesh: prompt: 32 (over y, x), comp: 16 (over z, core).
Axes of the slice: x: 4, y: 8, z: 8, core: 2. Of those that a mesh axis runs over, the one named last changes fastest.
Arguments:
- queries: bfloat16 [16, 4096, 4096], P('comp', 'prompt')
- grad_out: bfloat16 [16, 4096, 4096], P('comp', 'prompt'), may hold values from -24 to 24
- outputs: bfloat16 [16, 4096, 4096], P('comp', 'prompt'), may hold values from -0.59765625 to 0.59765625
- completion_log_sum_exp: float32 [16, 32, 4096], P('comp', None, 'prompt'), may hold values from 7 to 11
- lengths: int32 [16], P('comp'), may hold values from 1 to 4096, 32768 in all
- shared_prompt_keys: bfloat16 [256, 512], P('prompt')
- shared_prompt_values: bfloat16 [256, 512], P('prompt'), may hold values from -0.5 to 0.5
Outputs:
- query_row_gradients: bfloat16 [16, 4096, 4096], P('comp', 'prompt')
- grad_prompt_keys: bfloat16 [256, 512], P('prompt')
- grad_prompt_values: bfloat16 [256, 512], P('prompt')
The draws below stay inside these ranges and needn't reach their ends.
Inputs may be any that keep to these rules, and one draw needn't show every extreme that they name: `lengths`: one completion has length 4096.
All inputs are finite; a program needn't handle non-finite values. No bound on the sum of `lengths` on one device may be relied on, other than what follows from the above.
Results may differ from the reference program's by a relative error of at most 0.0054.
Values may be sent and summed in bfloat16 or wider, within the bound.
No kernel may reach another device: no remote copies, remote signals or barrier semaphores. Data moves between devices by JAX's collectives and lax.ppermute only.
A program may use at most 64 MiB of HBM per device.

```python
import math
import jax
import jax.numpy as jnp
import numpy as np
from jax import lax

QUERY_HEADS = 32
KEY_VALUE_HEADS = 4
HEAD_SIZE = 128
GROUP_COMPLETES = 16
COMPLETION_SLOTS = 4096
PROMPT_COUNT = 256


def key_table(key):
    return jax.random.normal(key, (PROMPT_COUNT, KEY_VALUE_HEADS * HEAD_SIZE), jnp.float32)


def draw_shared_prompt_keys(key, part):
    lookup_grid = key_table(key)
    return lookup_grid.astype(jnp.bfloat16)


def draw_queries(key, part):
    key = jax.random.fold_in(key, 23)
    first = jax.random.fold_in(key, 0)
    base = 2.0 * jax.random.normal(first, (GROUP_COMPLETES, COMPLETION_SLOTS, QUERY_HEADS * HEAD_SIZE), jnp.float32)
    return base.astype(jnp.bfloat16)


def levels(key, extent, cuts, least, high):
    def one(axis_at, shards_of):
        steps = jax.random.uniform(jax.random.fold_in(jax.random.fold_in(key, 6), axis_at), (shards_of,), jnp.float32, least / len(cuts), high / len(cuts))
        return jnp.repeat(jnp.exp(steps), extent[axis_at] // shards_of).reshape((-1,) + (1,) * (len(extent) - axis_at - 1))

    level = one(*cuts[0])
    for cut in cuts[1:]:
        level = level * one(*cut)
    return level


def split_up(number_of, total, most, skew):
    portions = [(1 << 20) // math.isqrt(standing ** skew) + 1 for standing in range(2, number_of + 1)]
    spare, given = total - most - (number_of - 1), [1] * (number_of - 1)
    while spare > 0:
        free = [i for i in range(number_of - 1) if given[i] < most]
        pool, left = sum([portions[i] for i in free]), spare
        for i in free:
            more = min(most - given[i], max(1, left * portions[i] // pool), spare)
            given[i] = given[i] + more
            spare = spare - more
    return np.array([most] + given)


def ragged_sizes(stream_key, number_of, total, reach, lean):
    if number_of == 2:
        one = jax.random.randint(stream_key, (), max(1, total - reach), min(reach, total - 1) + 1)
        return jnp.stack([one, total - one])
    sizes = jnp.asarray(split_up(number_of, total, reach, lean), jnp.int32)
    pairs = (number_of - 1) // 2
    giver, receiver = sizes[1:1 + 2 * pairs:2], sizes[2:2 + 2 * pairs:2]
    margin = jnp.minimum(giver - 1, reach - receiver)
    passed = jax.random.randint(jax.random.fold_in(stream_key, 1), (pairs,), 0, 1 << 20) % (margin + 1)
    sizes = sizes.at[1:1 + 2 * pairs:2].set(giver - passed).at[2:2 + 2 * pairs:2].set(receiver + passed)
    return sizes[jax.random.permutation(jax.random.fold_in(stream_key, 2), number_of)]


def scatter_about(rng, dims, width, bound, cuts=(), kind=jnp.bfloat16):
    drawn = width * jax.random.normal(rng, dims, jnp.float32)
    if cuts:
        drawn = drawn * levels(rng, dims, cuts, -0.22, 0.18)
    return jnp.clip(drawn, -bound, bound).astype(kind)


def setup_inputs(seed: int = 0) -> dict:
    streams_of = jax.random.split(jax.random.key(seed), 8)
    return {
        "queries": draw_queries(jax.random.fold_in(streams_of[7], 71), 0),
        "grad_out": scatter_about(streams_of[1], (GROUP_COMPLETES, COMPLETION_SLOTS, QUERY_HEADS * HEAD_SIZE), 4.0, 24.0, ((0, 16), (1, 32))),
        "outputs": scatter_about(streams_of[2], (GROUP_COMPLETES, COMPLETION_SLOTS, QUERY_HEADS * HEAD_SIZE), 0.1, 0.59765625, ((0, 16), (1, 32))),
        "completion_log_sum_exp": jnp.clip(7.0 + 4.0 * jax.random.uniform(streams_of[3], (GROUP_COMPLETES, QUERY_HEADS, COMPLETION_SLOTS), jnp.float32) ** levels(streams_of[3], (GROUP_COMPLETES, QUERY_HEADS, COMPLETION_SLOTS), ((0, 16), (2, 32)), -0.2, 0.2), 7.0, 11.0),
        "lengths": ragged_sizes(streams_of[4], GROUP_COMPLETES, GROUP_COMPLETES * COMPLETION_SLOTS // 2, COMPLETION_SLOTS, 2).astype(jnp.int32),
        "shared_prompt_keys": draw_shared_prompt_keys(jax.random.fold_in(streams_of[7], 71), 0),
        "shared_prompt_values": scatter_about(streams_of[6], (PROMPT_COUNT, KEY_VALUE_HEADS * HEAD_SIZE), HEAD_SIZE ** -0.5, 0.5, ((0, 32),)),
    }


def reference(queries, grad_out, outputs, completion_log_sum_exp, lengths, shared_prompt_keys, shared_prompt_values):
    scale = 1.0 / (HEAD_SIZE ** 0.5)
    query_group = QUERY_HEADS // KEY_VALUE_HEADS
    positions = jnp.arange(COMPLETION_SLOTS, dtype=jnp.int32)
    live = positions[None, :] < lengths[:, None]
    masked_scores = grad_out * live[:, :, None].astype(jnp.bfloat16)
    query_block_list = queries.reshape(GROUP_COMPLETES, COMPLETION_SLOTS, KEY_VALUE_HEADS, query_group, HEAD_SIZE)
    gradient_block_list = masked_scores.reshape(GROUP_COMPLETES, COMPLETION_SLOTS, KEY_VALUE_HEADS, query_group, HEAD_SIZE)
    output_block_list = outputs.reshape(GROUP_COMPLETES, COMPLETION_SLOTS, KEY_VALUE_HEADS, query_group, HEAD_SIZE)
    remaining_blocks = completion_log_sum_exp.reshape(GROUP_COMPLETES, KEY_VALUE_HEADS, query_group, COMPLETION_SLOTS)
    heads_of_keys = shared_prompt_keys.reshape(PROMPT_COUNT, KEY_VALUE_HEADS, HEAD_SIZE)
    heads_of_values = shared_prompt_values.reshape(PROMPT_COUNT, KEY_VALUE_HEADS, HEAD_SIZE)

    def single_block(loop_index):
        completion_number = loop_index // KEY_VALUE_HEADS
        head_number = loop_index % KEY_VALUE_HEADS
        q_part = query_block_list[completion_number, :, head_number].astype(jnp.float32)
        g_part = gradient_block_list[completion_number, :, head_number].astype(jnp.float32)
        o_part = output_block_list[completion_number, :, head_number].astype(jnp.float32)
        rest = remaining_blocks[completion_number, head_number]
        k_part = heads_of_keys[:, head_number].astype(jnp.float32)
        v_part = heads_of_values[:, head_number].astype(jnp.float32)
        scores = jnp.einsum('rhd,pd->hrp', q_part, k_part) * scale
        total = jnp.logaddexp(rest, jax.nn.logsumexp(scores, axis=-1))
        probs = jnp.exp(scores - total[:, :, None])
        probs_low = probs.astype(jnp.bfloat16).astype(jnp.float32)
        delta = jnp.einsum('rhd,rhd->hr', g_part, o_part)
        dprobs = jnp.einsum('rhd,pd->hrp', g_part, v_part)
        dscores = (probs * (dprobs - delta[:, :, None])).astype(jnp.bfloat16).astype(jnp.float32)
        query_gradient = jnp.einsum('hrp,pd->rhd', dscores, k_part) * scale
        key_gradient = jnp.einsum('hrp,rhd->pd', dscores, q_part) * scale
        value_gradient = jnp.einsum('hrp,rhd->pd', probs_low, g_part)
        return query_gradient, key_gradient, value_gradient

    query_gradient, key_gradient, value_gradient = lax.map(single_block, jnp.arange(GROUP_COMPLETES * KEY_VALUE_HEADS, dtype=jnp.int32))
    query_gradient = query_gradient.reshape(GROUP_COMPLETES, KEY_VALUE_HEADS, COMPLETION_SLOTS, query_group, HEAD_SIZE).transpose(0, 2, 1, 3, 4)
    query_row_gradients = query_gradient.reshape(GROUP_COMPLETES, COMPLETION_SLOTS, QUERY_HEADS * HEAD_SIZE).astype(jnp.bfloat16)
    key_gradient = jnp.sum(key_gradient.reshape(GROUP_COMPLETES, KEY_VALUE_HEADS, PROMPT_COUNT, HEAD_SIZE), axis=0).transpose(1, 0, 2)
    value_gradient = jnp.sum(value_gradient.reshape(GROUP_COMPLETES, KEY_VALUE_HEADS, PROMPT_COUNT, HEAD_SIZE), axis=0).transpose(1, 0, 2)
    return (query_row_gradients, key_gradient.reshape(PROMPT_COUNT, KEY_VALUE_HEADS * HEAD_SIZE).astype(jnp.bfloat16),
            value_gradient.reshape(PROMPT_COUNT, KEY_VALUE_HEADS * HEAD_SIZE).astype(jnp.bfloat16))
```

```python
import jax
import jax.numpy as jnp
from jax import lax
from jax.experimental import pallas as pl
from jax.experimental.pallas import tpu as pltpu
from jax.sharding import PartitionSpec as P

HEAD_SIZE = 128
LOG2_E = 1.4426950408889634


def rows_by_rows(a, b):
    return lax.dot_general(a, b, (((1,), (1,)), ((), ())), preferred_element_type=jnp.float32)


def columns_by_columns(a, b):
    return lax.dot_general(a, b, (((0,), (0,)), ((), ())), preferred_element_type=jnp.float32)


def attention_backward(live_ref, q_ref, g_ref, o_ref, rest_ref, k_ref, v_ref, dq_ref, dkv_ref):
    head = pl.program_id(0)
    rows = q_ref.shape[0]
    heads = q_ref.shape[1] // HEAD_SIZE
    kv_width = dkv_ref.shape[1] // 2
    scale = 1.0 / HEAD_SIZE**0.5
    live = lax.broadcasted_iota(jnp.int32, (rows, HEAD_SIZE), 0) < live_ref[0]
    keys = k_ref[...]
    values = v_ref[...]
    ones = jnp.ones((8, HEAD_SIZE), jnp.bfloat16)
    key_terms = jnp.zeros((keys.shape[0], HEAD_SIZE), jnp.float32)
    value_terms = jnp.zeros((keys.shape[0], HEAD_SIZE), jnp.float32)
    step = 2
    for first in range(0, heads, step):
        cut = [slice((first + i) * HEAD_SIZE, (first + i + 1) * HEAD_SIZE) for i in range(step)]
        q = jnp.concatenate([q_ref[:, c] for c in cut], axis=0)
        g = jnp.concatenate(
            [jnp.where(live, g_ref[:, c], jnp.zeros((), jnp.bfloat16)) for c in cut], axis=0
        )
        o = jnp.concatenate([o_ref[:, c] for c in cut], axis=0)
        rest = jnp.concatenate([rest_ref[first + i : first + i + 1, :] for i in range(step)], axis=1)
        rest = rest * LOG2_E
        scores = rows_by_rows(keys, q)
        top = jnp.maximum(jnp.max(scores, axis=0, keepdims=True) * (scale * LOG2_E), rest)
        weights = jnp.exp2(scores * (scale * LOG2_E) - top)
        total = jnp.sum(weights, axis=0, keepdims=True) + jnp.exp2(rest - top)
        probs = weights * (1.0 / total)
        product = g.astype(jnp.float32) * o.astype(jnp.float32)
        high = product.astype(jnp.bfloat16)
        low = (product - high.astype(jnp.float32)).astype(jnp.bfloat16)
        delta = (rows_by_rows(ones, high) + rows_by_rows(ones, low))[0:1]
        dprobs = rows_by_rows(values, g)
        dscores = (probs * (dprobs - delta)).astype(jnp.bfloat16)
        dq = (columns_by_columns(dscores, keys) * scale).astype(jnp.bfloat16)
        for i, c in enumerate(cut):
            dq_ref[:, c] = dq[i * rows : (i + 1) * rows]
        key_terms += jnp.dot(dscores, q, preferred_element_type=jnp.float32)
        value_terms += jnp.dot(
            probs.astype(jnp.bfloat16), g, preferred_element_type=jnp.float32
        )
    at = pl.multiple_of(head * HEAD_SIZE, HEAD_SIZE)
    dkv_ref[:, pl.ds(at, HEAD_SIZE)] = (key_terms * scale).astype(dkv_ref.dtype)
    dkv_ref[:, pl.ds(kv_width + at, HEAD_SIZE)] = value_terms.astype(dkv_ref.dtype)


def local_gradients(live, queries, grad_out, outputs, rest, kv):
    rows, width = queries.shape
    heads = rest.shape[0]
    prompt = kv.shape[0]
    kv_heads = kv.shape[1] // (2 * HEAD_SIZE)
    wide = width // kv_heads
    by_head = pl.BlockSpec((rows, wide), lambda h, live: (0, h))
    return pl.pallas_call(
        attention_backward,
        grid_spec=pltpu.PrefetchScalarGridSpec(
            num_scalar_prefetch=1,
            grid=(kv_heads,),
            in_specs=[
                by_head,
                by_head,
                by_head,
                pl.BlockSpec((heads // kv_heads, rows), lambda h, live: (h, 0)),
                pl.BlockSpec((prompt, HEAD_SIZE), lambda h, live: (0, h)),
                pl.BlockSpec((prompt, HEAD_SIZE), lambda h, live: (0, kv_heads + h)),
            ],
            out_specs=[by_head, pl.BlockSpec(kv.shape, lambda h, live: (0, 0))],
        ),
        out_shape=[
            jax.ShapeDtypeStruct(queries.shape, jnp.bfloat16),
            jax.ShapeDtypeStruct(kv.shape, jnp.bfloat16),
        ],
        compiler_params=pltpu.CompilerParams(
            dimension_semantics=("arbitrary",), vmem_limit_bytes=32 * 1024 * 1024
        ),
        name="attention_backward",
    )(live, queries, grad_out, outputs, rest, kv, kv)


def shards(
    queries,
    grad_out,
    outputs,
    completion_log_sum_exp,
    lengths,
    shared_prompt_keys,
    shared_prompt_values,
):
    rows = queries.shape[1]
    own, kv_width = shared_prompt_keys.shape
    owners = lax.axis_size("prompt")
    members = lax.axis_size("comp")
    kv_own = jnp.concatenate([shared_prompt_keys, shared_prompt_values], axis=1)
    kv_all = lax.all_to_all(
        jnp.broadcast_to(kv_own[None], (owners, own, 2 * kv_width)), "prompt", 0, 0
    )
    live = lengths - lax.axis_index("prompt") * rows
    grad_rows, terms = local_gradients(
        live,
        queries[0],
        grad_out[0],
        outputs[0],
        completion_log_sum_exp[0],
        kv_all.reshape(owners * own, 2 * kv_width),
    )
    shares = lax.all_to_all(terms.reshape(owners, own, 2 * kv_width), "prompt", 0, 0)
    share = jnp.sum(shares.astype(jnp.float32), axis=0).astype(jnp.bfloat16)
    parts = lax.all_to_all(
        jnp.broadcast_to(share[None], (members, own, 2 * kv_width)), "comp", 0, 0
    )
    total = jnp.sum(parts.astype(jnp.float32), axis=0).astype(jnp.bfloat16)
    return (grad_rows[None], total[:, :kv_width], total[:, kv_width:])


def solution(mesh):
    in_specs = (
        P("comp", "prompt", None),
        P("comp", "prompt", None),
        P("comp", "prompt", None),
        P("comp", None, "prompt"),
        P("comp"),
        P("prompt", None),
        P("prompt", None),
    )
    out_specs = (P("comp", "prompt", None), P("prompt", None), P("prompt", None))
    return jax.shard_map(shards, mesh=mesh, in_specs=in_specs, out_specs=out_specs, check_vma=False)
```

```python
import functools

import jax
import jax.numpy as jnp
from jax import lax
from jax.experimental import pallas as pl
from jax.experimental.pallas import tpu as pltpu
from jax.sharding import PartitionSpec as P

HEAD_SIZE = 128
LOG2_E = 1.4426950408889634
CORES = 2
SMALL_VMEM = 8 * 1024 * 1024


def rows_by_rows(a, b):
    return lax.dot_general(a, b, (((1,), (1,)), ((), ())), preferred_element_type=jnp.float32)


def spread_kernel(core_ref, k_ref, v_ref, out_ref):
    half = k_ref.shape[1] // CORES
    at = pl.ds(pl.multiple_of(core_ref[0] * half, half), half)
    both = jnp.concatenate([k_ref[:, at], v_ref[:, at]], axis=1)
    for i in range(out_ref.shape[0]):
        out_ref[i] = both


def spread(core, keys, values, owners):
    own, width = keys.shape
    vmem = pl.BlockSpec(memory_space=pltpu.VMEM)
    return pl.pallas_call(
        spread_kernel,
        in_specs=[pl.BlockSpec(memory_space=pltpu.SMEM), vmem, vmem],
        out_specs=vmem,
        out_shape=jax.ShapeDtypeStruct((owners, own, 2 * width // CORES), keys.dtype),
        compiler_params=pltpu.CompilerParams(vmem_limit_bytes=SMALL_VMEM),
        name="spread",
    )(core, keys, values)


def delta_kernel(live_ref, g_ref, o_ref, delta_ref):
    rows, wide = o_ref.shape
    heads = wide // HEAD_SIZE
    step = pl.program_id(0)
    live = lax.broadcasted_iota(jnp.int32, (rows, HEAD_SIZE), 0) < live_ref[0]
    columns = []
    for h in range(heads):
        cut = slice(h * HEAD_SIZE, (h + 1) * HEAD_SIZE)
        at = pl.ds(pl.multiple_of(step * wide + h * HEAD_SIZE, HEAD_SIZE), HEAD_SIZE)
        product = g_ref[:, at].astype(jnp.float32) * o_ref[:, cut].astype(jnp.float32)
        columns.append(jnp.sum(jnp.where(live, product, 0.0), axis=1, keepdims=True))
    own = pl.ds(pl.multiple_of(step * heads, heads), heads)
    delta_ref[own, :] = jnp.concatenate(columns, axis=1).T


def row_delta(live, grad_out, outputs, heads, steps):
    rows, width = grad_out.shape
    vmem = pl.BlockSpec(memory_space=pltpu.VMEM)
    return pl.pallas_call(
        delta_kernel,
        grid=(steps,),
        in_specs=[
            pl.BlockSpec(memory_space=pltpu.SMEM),
            vmem,
            pl.BlockSpec((rows, width // steps), lambda h: (0, h)),
        ],
        out_specs=vmem,
        out_shape=jax.ShapeDtypeStruct((heads, rows), jnp.float32),
        cost_estimate=pl.CostEstimate(
            flops=3 * rows * width, bytes_accessed=4 * rows * width, transcendentals=0
        ),
        compiler_params=pltpu.CompilerParams(vmem_limit_bytes=SMALL_VMEM),
        name="delta",
    )(live, grad_out, outputs)


def backward_kernel(group, place_ref, q_ref, g_ref, rest_ref, delta_ref, kv_ref, *refs):
    dq_hbm, dkv_ref, dq_buf, out_sem = refs[-4:]
    steps, rows, wide = dq_buf.shape
    half = dkv_ref.shape[1] // 2
    scale = 1.0 / HEAD_SIZE**0.5
    first = place_ref[1] * steps
    live = lax.broadcasted_iota(jnp.int32, (rows, HEAD_SIZE), 0) < place_ref[0]
    stores = []
    for i in range(steps):
        keys = kv_ref[:, i * HEAD_SIZE : (i + 1) * HEAD_SIZE]
        values = kv_ref[:, half + i * HEAD_SIZE : half + (i + 1) * HEAD_SIZE]
        own = pl.ds(pl.multiple_of((first + i) * group, group), group)
        rest_rows = rest_ref[own, :] * LOG2_E
        delta_rows = delta_ref[own, :]
        rest = jnp.concatenate([rest_rows[h : h + 1] for h in range(group)], axis=1)
        delta = jnp.concatenate([delta_rows[h : h + 1] for h in range(group)], axis=1)
        at = pl.multiple_of((first + i) * wide, wide)
        columns = [pl.ds(at + h * HEAD_SIZE, HEAD_SIZE) for h in range(group)]
        q = jnp.concatenate([q_ref[:, cut] for cut in columns], axis=0)
        g = jnp.concatenate(
            [jnp.where(live, g_ref[:, cut], jnp.zeros((), jnp.bfloat16)) for cut in columns], axis=0
        )
        scores = rows_by_rows(keys, q)
        top = jnp.maximum(jnp.max(scores, axis=0, keepdims=True) * (scale * LOG2_E), rest)
        weights = jnp.exp2(scores * (scale * LOG2_E) - top)
        total = jnp.sum(weights, axis=0, keepdims=True) + jnp.exp2(rest - top)
        probs = weights * (1.0 / total)
        dprobs = rows_by_rows(values, g)
        dscores = (probs * (dprobs - delta)).astype(jnp.bfloat16)
        dq = jnp.dot(keys.T, dscores, preferred_element_type=jnp.float32) * scale
        dq = dq.astype(jnp.bfloat16)
        for h in range(group):
            dq_buf[i, :, h * HEAD_SIZE : (h + 1) * HEAD_SIZE] = dq[:, h * rows : (h + 1) * rows].T
        store = pltpu.make_async_copy(dq_buf.at[i], dq_hbm.at[:, pl.ds(at, wide)], out_sem.at[i])
        store.start()
        stores.append(store)
        key_terms = jnp.dot(dscores, q, preferred_element_type=jnp.float32) * scale
        value_terms = jnp.dot(probs.astype(jnp.bfloat16), g, preferred_element_type=jnp.float32)
        dkv_ref[:, i * HEAD_SIZE : (i + 1) * HEAD_SIZE] = key_terms.astype(dkv_ref.dtype)
        dkv_ref[:, half + i * HEAD_SIZE : half + (i + 1) * HEAD_SIZE] = value_terms.astype(
            dkv_ref.dtype
        )
    for store in stores:
        store.wait()


def half_gradients(place, queries, grad_out, rest, delta, kv, dtype, grad_rows=None):
    rows, width = queries.shape
    heads = rest.shape[0]
    prompt, columns = kv.shape
    steps = columns // (2 * HEAD_SIZE)
    wide = width // (CORES * steps)
    hbm = pl.BlockSpec(memory_space=pltpu.HBM)
    vmem = pl.BlockSpec(memory_space=pltpu.VMEM)
    operands = [place, queries, grad_out, rest, delta, kv]
    in_specs = [pl.BlockSpec(memory_space=pltpu.SMEM)] + [vmem] * 5
    aliases = {}
    if grad_rows is not None:
        operands.append(grad_rows)
        in_specs.append(hbm)
        aliases = {6: 0}
    products = rows * (heads // CORES) * prompt
    return pl.pallas_call(
        functools.partial(backward_kernel, wide // HEAD_SIZE),
        in_specs=in_specs,
        out_specs=[hbm, vmem],
        out_shape=[
            jax.ShapeDtypeStruct(queries.shape, queries.dtype),
            jax.ShapeDtypeStruct(kv.shape, dtype),
        ],
        scratch_shapes=[
            pltpu.VMEM((steps, rows, wide), queries.dtype),
            pltpu.SemaphoreType.DMA((steps,)),
        ],
        input_output_aliases=aliases,
        compiler_params=pltpu.CompilerParams(vmem_limit_bytes=40 * 1024 * 1024),
        cost_estimate=pl.CostEstimate(
            flops=10 * products * HEAD_SIZE, bytes_accessed=3 * rows * width, transcendentals=products
        ),
        name="attention_backward",
    )(*operands)


def finish_kernel(parts_ref, key_ref, value_ref):
    half = parts_ref.shape[2] // 2
    for core in range(CORES):
        total = parts_ref[core].astype(jnp.float32)
        for i in range(core + CORES, parts_ref.shape[0], CORES):
            total += parts_ref[i].astype(jnp.float32)
        at = slice((CORES - 1 - core) * half, (CORES - core) * half)
        key_ref[:, at] = total[:, :half].astype(key_ref.dtype)
        value_ref[:, at] = total[:, half:].astype(value_ref.dtype)


def finish(parts, like):
    return pl.pallas_call(
        finish_kernel,
        in_specs=[pl.BlockSpec(memory_space=pltpu.VMEM)],
        out_shape=[jax.ShapeDtypeStruct(like.shape, like.dtype)] * 2,
        compiler_params=pltpu.CompilerParams(vmem_limit_bytes=SMALL_VMEM),
        name="finish",
    )(parts)


def shards(
    queries,
    grad_out,
    outputs,
    completion_log_sum_exp,
    lengths,
    shared_prompt_keys,
    shared_prompt_values,
):
    rows = queries.shape[1]
    own, kv_width = shared_prompt_keys.shape
    heads = completion_log_sum_exp.shape[1]
    owners = lax.axis_size("prompt")
    members = lax.axis_size("comp")
    other_core = [(i, i ^ 1) for i in range(members)]
    core = lax.rem(lax.axis_index("comp"), CORES).astype(jnp.int32)
    live = lengths - lax.axis_index("prompt") * rows
    mine = jnp.concatenate([live, core[None]])
    others = jnp.concatenate([live, 1 - core[None]])
    rest = completion_log_sum_exp[0]

    near = lax.all_to_all(
        spread(core[None], shared_prompt_keys, shared_prompt_values, owners), "prompt", 0, 0
    ).reshape(owners * own, kv_width)
    delta = row_delta(live, grad_out[0], outputs[0], heads, kv_width // HEAD_SIZE)
    far = lax.ppermute(near, "comp", other_core)
    grad_rows, sent = half_gradients(
        mine, queries[0], grad_out[0], rest, delta, near, jnp.bfloat16
    )
    received = lax.ppermute(sent, "comp", other_core)
    grad_rows, kept = half_gradients(
        others, queries[0], grad_out[0], rest, delta, far, jnp.float32, grad_rows
    )
    terms = (kept + received.astype(jnp.float32)).astype(jnp.bfloat16)
    shares = lax.all_to_all(terms.reshape(owners, own, kv_width), "prompt", 0, 0)
    share = jnp.sum(shares.astype(jnp.float32), axis=0).astype(jnp.bfloat16)
    parts = lax.all_to_all(
        jnp.broadcast_to(share[None], (members, own, kv_width)), "comp", 0, 0
    )
    key_out, value_out = finish(parts, shared_prompt_keys)
    return (grad_rows[None], key_out, value_out)


def solution(mesh):
    in_specs = (
        P("comp", "prompt", None),
        P("comp", "prompt", None),
        P("comp", "prompt", None),
        P("comp", None, "prompt"),
        P("comp"),
        P("prompt", None),
        P("prompt", None),
    )
    out_specs = (P("comp", "prompt", None), P("prompt", None), P("prompt", None))
    return jax.shard_map(shards, mesh=mesh, in_specs=in_specs, out_specs=out_specs, check_vma=False)
```

```python
import functools

import jax
import jax.numpy as jnp
from jax import lax
from jax.experimental import pallas as pl
from jax.experimental.pallas import tpu as pltpu
from jax.sharding import PartitionSpec as P

HEAD_SIZE = 128
LOG2_E = 1.4426950408889634
CORES = 2
SMALL_VMEM = 8 * 1024 * 1024
LARGE_VMEM = 24 * 1024 * 1024
FULL_VMEM = 56 * 1024 * 1024
PIECES = 4


def rows_by_rows(a, b):
    return lax.dot_general(a, b, (((1,), (1,)), ((), ())), preferred_element_type=jnp.float32)


def own_core():
    return lax.rem(lax.axis_index("comp"), CORES)


def spread_kernel(k_hbm, v_hbm, out_hbm, half_buf, out_buf, in_sems, out_sems):
    half = half_buf.shape[2]
    at = pl.ds(pl.multiple_of(own_core() * half, half), half)
    loads = [
        pltpu.make_async_copy(ref.at[:, at], half_buf.at[i], in_sems.at[i])
        for i, ref in enumerate((k_hbm, v_hbm))
    ]
    for copy in loads:
        copy.start()
    for copy in loads:
        copy.wait()
    both = jnp.concatenate([half_buf[0], half_buf[1]], axis=1)
    pieces = out_sems.shape[0]
    piece = out_buf.shape[0] // pieces
    stores = []
    for i in range(pieces):
        for j in range(piece):
            out_buf[i * piece + j] = both
        own = pl.ds(i * piece, piece)
        stores.append(pltpu.make_async_copy(out_buf.at[own], out_hbm.at[own], out_sems.at[i]))
        stores[-1].start()
    for copy in stores:
        copy.wait()


def spread(keys, values, owners):
    own, width = keys.shape
    hbm = pl.BlockSpec(memory_space=pltpu.HBM)
    shape = (owners, own, 2 * width // CORES)
    return pl.pallas_call(
        spread_kernel,
        in_specs=[hbm, hbm],
        out_specs=hbm,
        out_shape=jax.ShapeDtypeStruct(shape, keys.dtype),
        scratch_shapes=[
            pltpu.VMEM((2, own, width // CORES), keys.dtype),
            pltpu.VMEM(shape, keys.dtype),
            pltpu.SemaphoreType.DMA((2,)),
            pltpu.SemaphoreType.DMA((4,)),
        ],
        compiler_params=pltpu.CompilerParams(vmem_limit_bytes=FULL_VMEM),
        name="spread",
    )(keys, values)


def delta_kernel(live_ref, g_ref, o_ref, delta_ref, keep_ref):
    rows, wide = o_ref.shape
    heads = wide // HEAD_SIZE
    step = pl.program_id(0)
    live = lax.broadcasted_iota(jnp.int32, (rows, HEAD_SIZE), 0) < live_ref[0]
    keep_ref[...] = live.astype(jnp.float32)
    columns = []
    for h in range(heads):
        cut = slice(h * HEAD_SIZE, (h + 1) * HEAD_SIZE)
        at = pl.ds(pl.multiple_of(step * wide + h * HEAD_SIZE, HEAD_SIZE), HEAD_SIZE)
        product = g_ref[:, at].astype(jnp.float32) * o_ref[:, cut].astype(jnp.float32)
        columns.append(jnp.sum(jnp.where(live, product, 0.0), axis=1, keepdims=True))
    own = pl.ds(pl.multiple_of(step * heads, heads), heads)
    delta_ref[own, :] = jnp.concatenate(columns, axis=1).T


def row_delta(live, grad_out, outputs, heads, steps):
    rows, width = grad_out.shape
    vmem = pl.BlockSpec(memory_space=pltpu.VMEM)
    return pl.pallas_call(
        delta_kernel,
        grid=(steps,),
        in_specs=[
            pl.BlockSpec(memory_space=pltpu.SMEM),
            vmem,
            pl.BlockSpec((rows, width // steps), lambda h: (0, h)),
        ],
        out_specs=[vmem, vmem],
        out_shape=[
            jax.ShapeDtypeStruct((heads, rows), jnp.float32),
            jax.ShapeDtypeStruct((rows, HEAD_SIZE), jnp.float32),
        ],
        compiler_params=pltpu.CompilerParams(vmem_limit_bytes=SMALL_VMEM),
        cost_estimate=pl.CostEstimate(
            flops=3 * rows * width, bytes_accessed=4 * rows * width, transcendentals=0
        ),
        name="delta",
    )(live, grad_out, outputs)


def scores_and_dprobs(keys, values, q, g):
    return rows_by_rows(keys, q), rows_by_rows(values, g)


def probs_and_dscores(scores, dprobs, rest, delta):
    scale = LOG2_E / HEAD_SIZE**0.5
    rest = rest * LOG2_E
    top = jnp.maximum(jnp.max(scores, axis=0, keepdims=True) * scale, rest)
    weights = jnp.exp2(scores * scale - top)
    total = jnp.sum(weights, axis=0, keepdims=True) + jnp.exp2(rest - top)
    probs = weights * (1.0 / total)
    dscores = probs * (dprobs - delta)
    return probs.astype(jnp.bfloat16), dscores.astype(jnp.bfloat16)


def side_by_side(tile):
    return jnp.concatenate([tile[h : h + 1] for h in range(tile.shape[0])], axis=1)


def place_half(side, half_ref, rows_hbm, sems):
    width = half_ref.shape[1]
    pieces = sems.shape[0]
    piece = width // pieces
    copies = []
    for i in range(pieces):
        to = pl.ds(pl.multiple_of(side * width + i * piece, piece), piece)
        copies.append(
            pltpu.make_async_copy(
                half_ref.at[:, i * piece : (i + 1) * piece], rows_hbm.at[:, to], sems.at[i]
            )
        )
        copies[-1].start()
    return copies


def backward_kernel(turn, q_ref, g_ref, rest_ref, delta_ref, keep_ref, kv_ref, *refs):
    if turn == 0:
        dq_ref, dkv_ref = refs
    else:
        before_ref, dq_ref, dkv_ref, rows_hbm, sems = refs
    rows, width = dq_ref.shape
    half = dkv_ref.shape[1] // 2
    steps = half // HEAD_SIZE
    wide = width // steps
    group = wide // HEAD_SIZE
    scale = 1.0 / HEAD_SIZE**0.5
    side = own_core() if turn == 0 else 1 - own_core()
    first = side * steps
    copies = []
    if turn == 1:
        copies = place_half(own_core(), before_ref, rows_hbm, sems)
    keep = keep_ref[...]
    q, g, p, ds, held = {}, {}, {}, {}, {}
    for i in range(steps):
        at = pl.multiple_of((first + i) * wide, wide)
        columns = [pl.ds(at + h * HEAD_SIZE, HEAD_SIZE) for h in range(group)]
        q[i] = jnp.concatenate([q_ref[:, cut] for cut in columns], axis=0)
        g[i] = jnp.concatenate(
            [(g_ref[:, cut].astype(jnp.float32) * keep).astype(jnp.bfloat16) for cut in columns],
            axis=0,
        )
        key_at = slice(i * HEAD_SIZE, (i + 1) * HEAD_SIZE)
        value_at = slice(half + i * HEAD_SIZE, half + (i + 1) * HEAD_SIZE)
        held[i] = scores_and_dprobs(kv_ref[:, key_at], kv_ref[:, value_at], q[i], g[i])
    for i in range(steps):
        own = pl.ds(pl.multiple_of((first + i) * group, group), group)
        p[i], ds[i] = probs_and_dscores(
            *held[i], side_by_side(rest_ref[own, :]), side_by_side(delta_ref[own, :])
        )
        keys = kv_ref[:, i * HEAD_SIZE : (i + 1) * HEAD_SIZE]
        dq = jnp.dot(keys.T, ds[i], preferred_element_type=jnp.float32) * scale
        dq = dq.astype(jnp.bfloat16)
        for h in range(group):
            cut = slice(i * wide + h * HEAD_SIZE, i * wide + (h + 1) * HEAD_SIZE)
            dq_ref[:, cut] = dq[:, h * rows : (h + 1) * rows].T
    for i in range(steps):
        key_terms = jnp.dot(ds[i], q[i], preferred_element_type=jnp.float32) * scale
        value_terms = jnp.dot(p[i], g[i], preferred_element_type=jnp.float32)
        dkv_ref[:, i * HEAD_SIZE : (i + 1) * HEAD_SIZE] = key_terms.astype(dkv_ref.dtype)
        dkv_ref[:, half + i * HEAD_SIZE : half + (i + 1) * HEAD_SIZE] = value_terms.astype(
            dkv_ref.dtype
        )
    for copy in copies:
        copy.wait()


def half_gradients(turn, queries, grad_out, rest, delta, keep, kv, *before):
    rows, width = queries.shape
    products = rows * (rest.shape[0] // CORES) * kv.shape[0]
    vmem = pl.BlockSpec(memory_space=pltpu.VMEM)
    out_specs = [vmem, vmem]
    out_shape = [
        jax.ShapeDtypeStruct((rows, width // CORES), queries.dtype),
        jax.ShapeDtypeStruct(kv.shape, jnp.float32 if turn else jnp.bfloat16),
    ]
    scratch = []
    if turn == 1:
        out_specs.append(pl.BlockSpec(memory_space=pltpu.HBM))
        out_shape.append(jax.ShapeDtypeStruct(queries.shape, queries.dtype))
        scratch.append(pltpu.SemaphoreType.DMA((PIECES,)))
    return pl.pallas_call(
        functools.partial(backward_kernel, turn),
        in_specs=[vmem] * (6 + len(before)),
        out_specs=out_specs,
        out_shape=out_shape,
        scratch_shapes=scratch,
        compiler_params=pltpu.CompilerParams(vmem_limit_bytes=LARGE_VMEM),
        cost_estimate=pl.CostEstimate(
            flops=10 * products * HEAD_SIZE, bytes_accessed=3 * rows * width, transcendentals=products
        ),
        name="attention_backward",
    )(queries, grad_out, rest, delta, keep, kv, *before)


def finish_kernel(
    parts_ref, far_ref, before_hbm, key_hbm, value_hbm, rows_hbm, key_buf, value_buf, sems, out_sems
):
    copies = place_half(1 - own_core(), far_ref, rows_hbm, sems)
    half = parts_ref.shape[2] // 2
    for core in range(CORES):
        total = parts_ref[core].astype(jnp.float32)
        for i in range(core + CORES, parts_ref.shape[0], CORES):
            total += parts_ref[i].astype(jnp.float32)
        at = slice((CORES - 1 - core) * half, (CORES - core) * half)
        key_buf[:, at] = total[:, :half].astype(key_buf.dtype)
        value_buf[:, at] = total[:, half:].astype(value_buf.dtype)
    for i, (buf, hbm) in enumerate(((key_buf, key_hbm), (value_buf, value_hbm))):
        copies.append(pltpu.make_async_copy(buf, hbm, out_sems.at[i]))
        copies[-1].start()
    for copy in copies:
        copy.wait()


def finish(parts, far, grad_rows, like):
    vmem = pl.BlockSpec(memory_space=pltpu.VMEM)
    hbm = pl.BlockSpec(memory_space=pltpu.HBM)
    one = jax.ShapeDtypeStruct(like.shape, like.dtype)
    return pl.pallas_call(
        finish_kernel,
        in_specs=[vmem, vmem, hbm],
        out_specs=[hbm, hbm, hbm],
        out_shape=[one, one, jax.ShapeDtypeStruct(grad_rows.shape, grad_rows.dtype)],
        scratch_shapes=[
            pltpu.VMEM(like.shape, like.dtype),
            pltpu.VMEM(like.shape, like.dtype),
            pltpu.SemaphoreType.DMA((PIECES,)),
            pltpu.SemaphoreType.DMA((2,)),
        ],
        input_output_aliases={2: 2},
        compiler_params=pltpu.CompilerParams(vmem_limit_bytes=SMALL_VMEM),
        name="finish",
    )(parts, far, grad_rows)


def shards(
    queries,
    grad_out,
    outputs,
    completion_log_sum_exp,
    lengths,
    shared_prompt_keys,
    shared_prompt_values,
):
    rows = queries.shape[1]
    own, kv_width = shared_prompt_keys.shape
    heads = completion_log_sum_exp.shape[1]
    owners = lax.axis_size("prompt")
    members = lax.axis_size("comp")
    other_core = [(i, i ^ 1) for i in range(members)]
    live = lengths - lax.axis_index("prompt") * rows
    rest = completion_log_sum_exp[0]

    near = lax.all_to_all(
        spread(shared_prompt_keys, shared_prompt_values, owners), "prompt", 0, 0
    ).reshape(owners * own, kv_width)
    delta, keep = row_delta(live, grad_out[0], outputs[0], heads, kv_width // HEAD_SIZE)
    far = lax.ppermute(near, "comp", other_core)
    grad_near, sent = half_gradients(0, queries[0], grad_out[0], rest, delta, keep, near)
    received = lax.ppermute(sent, "comp", other_core)
    grad_far, kept, grad_rows = half_gradients(
        1, queries[0], grad_out[0], rest, delta, keep, far, grad_near
    )
    terms = (kept + received.astype(jnp.float32)).astype(jnp.bfloat16)
    shares = lax.all_to_all(terms.reshape(owners, own, kv_width), "prompt", 0, 0)
    share = jnp.sum(shares.astype(jnp.float32), axis=0).astype(jnp.bfloat16)
    parts = lax.all_to_all(
        jnp.broadcast_to(share[None], (members, own, kv_width)), "comp", 0, 0
    )
    key_out, value_out, grad_rows = finish(parts, grad_far, grad_rows, shared_prompt_keys)
    return (grad_rows[None], key_out, value_out)


def solution(mesh):
    in_specs = (
        P("comp", "prompt", None),
        P("comp", "prompt", None),
        P("comp", "prompt", None),
        P("comp", None, "prompt"),
        P("comp"),
        P("prompt", None),
        P("prompt", None),
    )
    out_specs = (P("comp", "prompt", None), P("prompt", None), P("prompt", None))
    return jax.shard_map(shards, mesh=mesh, in_specs=in_specs, out_specs=out_specs, check_vma=False)
```

```python
import jax
import jax.numpy as jnp
from jax import lax
from jax.experimental import pallas as pl
from jax.experimental.pallas import tpu as pltpu
from jax.sharding import PartitionSpec as P

HEAD_SIZE = 128
SCALE = 1.0 / HEAD_SIZE**0.5
LOG2_E = 1.4426950408889634
CORES = 2
SMALL_VMEM = 8 * 1024 * 1024
LARGE_VMEM = 24 * 1024 * 1024
FULL_VMEM = 56 * 1024 * 1024
PIECES = 4


def rows_by_rows(a, b):
    return lax.dot_general(a, b, (((1,), (1,)), ((), ())), preferred_element_type=jnp.float32)


def own_core():
    return lax.rem(lax.axis_index("comp"), CORES)


def spread_kernel(k_hbm, v_hbm, out_hbm, half_buf, out_buf, in_sems, out_sems):
    half = half_buf.shape[2]
    at = pl.ds(pl.multiple_of(own_core() * half, half), half)
    loads = [
        pltpu.make_async_copy(ref.at[:, at], half_buf.at[i], in_sems.at[i])
        for i, ref in enumerate((k_hbm, v_hbm))
    ]
    for copy in loads:
        copy.start()
    for copy in loads:
        copy.wait()
    both = jnp.concatenate([half_buf[0], half_buf[1]], axis=1)
    pieces = out_sems.shape[0]
    piece = out_buf.shape[0] // pieces
    stores = []
    for i in range(pieces):
        for j in range(piece):
            out_buf[i * piece + j] = both
        own = pl.ds(i * piece, piece)
        stores.append(pltpu.make_async_copy(out_buf.at[own], out_hbm.at[own], out_sems.at[i]))
        stores[-1].start()
    for copy in stores:
        copy.wait()


def spread(keys, values, owners):
    own, width = keys.shape
    hbm = pl.BlockSpec(memory_space=pltpu.HBM)
    shape = (owners, own, 2 * width // CORES)
    return pl.pallas_call(
        spread_kernel,
        in_specs=[hbm, hbm],
        out_specs=hbm,
        out_shape=jax.ShapeDtypeStruct(shape, keys.dtype),
        scratch_shapes=[
            pltpu.VMEM((2, own, width // CORES), keys.dtype),
            pltpu.VMEM(shape, keys.dtype),
            pltpu.SemaphoreType.DMA((2,)),
            pltpu.SemaphoreType.DMA((4,)),
        ],
        compiler_params=pltpu.CompilerParams(vmem_limit_bytes=FULL_VMEM),
        name="spread",
    )(keys, values)


def delta_kernel(live_ref, g_ref, o_ref, delta_ref, keep_ref):
    rows, wide = o_ref.shape
    heads = wide // HEAD_SIZE
    step = pl.program_id(0)
    live = lax.broadcasted_iota(jnp.int32, (rows, HEAD_SIZE), 0) < live_ref[0]
    keep_ref[...] = live.astype(jnp.float32)
    columns = []
    for h in range(heads):
        cut = slice(h * HEAD_SIZE, (h + 1) * HEAD_SIZE)
        at = pl.ds(pl.multiple_of(step * wide + h * HEAD_SIZE, HEAD_SIZE), HEAD_SIZE)
        product = g_ref[:, at].astype(jnp.float32) * o_ref[:, cut].astype(jnp.float32)
        columns.append(jnp.sum(jnp.where(live, product, 0.0), axis=1, keepdims=True))
    own = pl.ds(pl.multiple_of(step * heads, heads), heads)
    delta_ref[own, :] = jnp.concatenate(columns, axis=1).T


def row_delta(live, grad_out, outputs, heads, steps):
    rows, width = grad_out.shape
    vmem = pl.BlockSpec(memory_space=pltpu.VMEM)
    return pl.pallas_call(
        delta_kernel,
        grid=(steps,),
        in_specs=[
            pl.BlockSpec(memory_space=pltpu.SMEM),
            vmem,
            pl.BlockSpec((rows, width // steps), lambda h: (0, h)),
        ],
        out_specs=[vmem, vmem],
        out_shape=[
            jax.ShapeDtypeStruct((heads, rows), jnp.float32),
            jax.ShapeDtypeStruct((rows, HEAD_SIZE), jnp.float32),
        ],
        compiler_params=pltpu.CompilerParams(vmem_limit_bytes=SMALL_VMEM),
        cost_estimate=pl.CostEstimate(
            flops=3 * rows * width, bytes_accessed=4 * rows * width, transcendentals=0
        ),
        name="delta",
    )(live, grad_out, outputs)


def scores_and_dprobs(keys, values, q, g):
    return rows_by_rows(keys, q), rows_by_rows(values, g)


def probs_and_dscores(scores, dprobs, rest, delta):
    scale = LOG2_E * SCALE
    rest = rest * LOG2_E
    top = jnp.maximum(jnp.max(scores, axis=0, keepdims=True) * scale, rest)
    weights = jnp.exp2(scores * scale - top)
    total = jnp.sum(weights, axis=0, keepdims=True) + jnp.exp2(rest - top)
    probs = weights * (1.0 / total)
    dscores = probs * (dprobs - delta)
    return probs.astype(jnp.bfloat16), dscores.astype(jnp.bfloat16)


def side_by_side(tile):
    return jnp.concatenate([tile[h : h + 1] for h in range(tile.shape[0])], axis=1)


def place_half(side, half_ref, rows_hbm, sems):
    width = half_ref.shape[1]
    pieces = sems.shape[0]
    piece = width // pieces
    copies = []
    for i in range(pieces):
        to = pl.ds(pl.multiple_of(side * width + i * piece, piece), piece)
        copies.append(
            pltpu.make_async_copy(
                half_ref.at[:, i * piece : (i + 1) * piece], rows_hbm.at[:, to], sems.at[i]
            )
        )
        copies[-1].start()
    return copies


def query_gradients(keys, dscores, rows, dq_ref, at):
    dq = jnp.dot(keys.T, dscores, preferred_element_type=jnp.float32) * SCALE
    dq = dq.astype(dq_ref.dtype)
    for h in range(dq.shape[1] // rows):
        cut = slice(at + h * HEAD_SIZE, at + (h + 1) * HEAD_SIZE)
        dq_ref[:, cut] = dq[:, h * rows : (h + 1) * rows].T


def key_cuts(width, steps):
    return [
        tuple(
            slice(side * width // 2 + i * HEAD_SIZE, side * width // 2 + (i + 1) * HEAD_SIZE)
            for side in range(2)
        )
        for i in range(steps)
    ]


def softmax_backward(side, steps, kv_ref, q_ref, g_ref, rest_ref, delta_ref, keep_ref):
    rows = q_ref.shape[0]
    wide = q_ref.shape[1] // (CORES * steps)
    group = wide // HEAD_SIZE
    first = side * steps
    keep = keep_ref[...]
    held = []
    for i, (key_at, value_at) in enumerate(key_cuts(kv_ref.shape[1], steps)):
        at = pl.multiple_of((first + i) * wide, wide)
        columns = [pl.ds(at + h * HEAD_SIZE, HEAD_SIZE) for h in range(group)]
        q = jnp.concatenate([q_ref[:, cut] for cut in columns], axis=0)
        g = jnp.concatenate(
            [(g_ref[:, cut].astype(jnp.float32) * keep).astype(jnp.bfloat16) for cut in columns],
            axis=0,
        )
        held.append((q, g, *scores_and_dprobs(kv_ref[:, key_at], kv_ref[:, value_at], q, g)))
    for i, (q, g, scores, dprobs) in enumerate(held):
        own = pl.ds(pl.multiple_of((first + i) * group, group), group)
        yield q, g, *probs_and_dscores(
            scores, dprobs, side_by_side(rest_ref[own, :]), side_by_side(delta_ref[own, :])
        )


def near_kernel(
    q_ref, g_ref, rest_ref, delta_ref, keep_ref, kv_ref, packet_ref, dscores_ref
):
    prompt, width = kv_ref.shape
    steps = width // (2 * HEAD_SIZE)
    wide = dscores_ref.shape[1] // steps
    packet_ref[:prompt, :] = kv_ref[...]
    parts = softmax_backward(
        own_core(), steps, kv_ref, q_ref, g_ref, rest_ref, delta_ref, keep_ref
    )
    for i, (q, g, probs, dscores) in enumerate(parts):
        key_at, value_at = key_cuts(width, steps)[i]
        dscores_ref[:, i * wide : (i + 1) * wide] = dscores
        key_terms = jnp.dot(dscores, q, preferred_element_type=jnp.float32) * SCALE
        value_terms = jnp.dot(probs, g, preferred_element_type=jnp.float32)
        packet_ref[prompt:, key_at] = key_terms.astype(packet_ref.dtype)
        packet_ref[prompt:, value_at] = value_terms.astype(packet_ref.dtype)


def near_rows_kernel(dscores_ref, kv_ref, dq_ref):
    rows, width = dq_ref.shape
    steps = kv_ref.shape[1] // (2 * HEAD_SIZE)
    wide = width // steps
    for i, (key_at, _) in enumerate(key_cuts(kv_ref.shape[1], steps)):
        dscores = dscores_ref[:, i * wide : (i + 1) * wide]
        query_gradients(kv_ref[:, key_at], dscores, rows, dq_ref, i * wide)


def far_kernel(
    q_ref,
    g_ref,
    rest_ref,
    delta_ref,
    keep_ref,
    packet_ref,
    near_ref,
    dq_ref,
    terms_ref,
    rows_hbm,
    sems,
):
    copies = place_half(own_core(), near_ref, rows_hbm, sems)
    prompt, width = terms_ref.shape
    rows = dq_ref.shape[0]
    steps = width // (2 * HEAD_SIZE)
    wide = dq_ref.shape[1] // steps
    kv_ref = packet_ref.at[:prompt, :]
    parts = softmax_backward(
        1 - own_core(), steps, kv_ref, q_ref, g_ref, rest_ref, delta_ref, keep_ref
    )
    for i, (q, g, probs, dscores) in enumerate(parts):
        key_at, value_at = key_cuts(width, steps)[i]
        query_gradients(kv_ref[:, key_at], dscores, rows, dq_ref, i * wide)
        key_terms = jnp.dot(dscores, q, preferred_element_type=jnp.float32) * SCALE
        value_terms = jnp.dot(probs, g, preferred_element_type=jnp.float32)
        terms_ref[:, key_at] = key_terms
        terms_ref[:, value_at] = value_terms
    for copy in copies:
        copy.wait()


def call(kernel, name, flops, out_shape, *operands, in_float32=(), in_hbm=(), scratch=()):
    vmem = pl.BlockSpec(memory_space=pltpu.VMEM)
    hbm = pl.BlockSpec(memory_space=pltpu.HBM)
    return pl.pallas_call(
        kernel,
        in_specs=[vmem] * len(operands),
        out_specs=[hbm if i in in_hbm else vmem for i in range(len(out_shape))],
        out_shape=[
            jax.ShapeDtypeStruct(shape, jnp.float32 if i in in_float32 else jnp.bfloat16)
            for i, shape in enumerate(out_shape)
        ],
        scratch_shapes=list(scratch),
        compiler_params=pltpu.CompilerParams(vmem_limit_bytes=LARGE_VMEM),
        cost_estimate=pl.CostEstimate(flops=flops, bytes_accessed=2**20, transcendentals=0),
        name=name,
    )(*operands)


def place_half(side, half_ref, rows_hbm, sems):
    width = half_ref.shape[1]
    pieces = sems.shape[0]
    piece = width // pieces
    copies = []
    for i in range(pieces):
        to = pl.ds(pl.multiple_of(side * width + i * piece, piece), piece)
        copies.append(
            pltpu.make_async_copy(
                half_ref.at[:, i * piece : (i + 1) * piece], rows_hbm.at[:, to], sems.at[i]
            )
        )
        copies[-1].start()
    return copies


def finish_kernel(
    parts_ref, far_ref, before_hbm, key_hbm, value_hbm, rows_hbm, key_buf, value_buf, sems, out_sems
):
    copies = place_half(1 - own_core(), far_ref, rows_hbm, sems)
    half = parts_ref.shape[2] // 2
    for core in range(CORES):
        total = parts_ref[core].astype(jnp.float32)
        for i in range(core + CORES, parts_ref.shape[0], CORES):
            total += parts_ref[i].astype(jnp.float32)
        at = slice((CORES - 1 - core) * half, (CORES - core) * half)
        key_buf[:, at] = total[:, :half].astype(key_buf.dtype)
        value_buf[:, at] = total[:, half:].astype(value_buf.dtype)
    for i, (buf, hbm) in enumerate(((key_buf, key_hbm), (value_buf, value_hbm))):
        copies.append(pltpu.make_async_copy(buf, hbm, out_sems.at[i]))
        copies[-1].start()
    for copy in copies:
        copy.wait()


def finish(parts, far, grad_rows, like):
    vmem = pl.BlockSpec(memory_space=pltpu.VMEM)
    hbm = pl.BlockSpec(memory_space=pltpu.HBM)
    one = jax.ShapeDtypeStruct(like.shape, like.dtype)
    return pl.pallas_call(
        finish_kernel,
        in_specs=[vmem, vmem, hbm],
        out_specs=[hbm, hbm, hbm],
        out_shape=[one, one, jax.ShapeDtypeStruct(grad_rows.shape, grad_rows.dtype)],
        scratch_shapes=[
            pltpu.VMEM(like.shape, like.dtype),
            pltpu.VMEM(like.shape, like.dtype),
            pltpu.SemaphoreType.DMA((PIECES,)),
            pltpu.SemaphoreType.DMA((2,)),
        ],
        input_output_aliases={2: 2},
        compiler_params=pltpu.CompilerParams(vmem_limit_bytes=SMALL_VMEM),
        name="finish",
    )(parts, far, grad_rows)


def shards(
    queries,
    grad_out,
    outputs,
    completion_log_sum_exp,
    lengths,
    shared_prompt_keys,
    shared_prompt_values,
):
    rows = queries.shape[1]
    own, kv_width = shared_prompt_keys.shape
    heads = completion_log_sum_exp.shape[1]
    owners = lax.axis_size("prompt")
    members = lax.axis_size("comp")
    other_core = [(i, i ^ 1) for i in range(members)]
    live = lengths - lax.axis_index("prompt") * rows
    rest = completion_log_sum_exp[0]

    near = lax.all_to_all(
        spread(shared_prompt_keys, shared_prompt_values, owners), "prompt", 0, 0
    ).reshape(owners * own, kv_width)
    delta, keep = row_delta(live, grad_out[0], outputs[0], heads, kv_width // HEAD_SIZE)
    width = queries.shape[2]
    half = (rows, width // CORES)
    prompt = near.shape[0]
    product = rows * width // CORES * prompt * 2
    given = (queries[0], grad_out[0], rest, delta, keep)
    packet, dscores = call(
        near_kernel,
        "near",
        4 * product,
        [(2 * prompt, kv_width), (prompt, width // CORES)],
        *given,
        near,
    )
    received = lax.ppermute(packet, "comp", other_core)
    (grad_near,) = call(near_rows_kernel, "near_rows", product, [half], dscores, near)
    grad_far, kept, grad_rows = call(
        far_kernel,
        "far",
        5 * product,
        [half, near.shape, (rows, width)],
        *given,
        received,
        grad_near,
        in_float32=(1,),
        in_hbm=(2,),
        scratch=[pltpu.SemaphoreType.DMA((PIECES,))],
    )
    terms = (kept + received[prompt:].astype(jnp.float32)).astype(jnp.bfloat16)
    shares = lax.all_to_all(terms.reshape(owners, own, kv_width), "prompt", 0, 0)
    share = jnp.sum(shares.astype(jnp.float32), axis=0).astype(jnp.bfloat16)
    parts = lax.all_to_all(
        jnp.broadcast_to(share[None], (members, own, kv_width)), "comp", 0, 0
    )
    key_out, value_out, grad_rows = finish(parts, grad_far, grad_rows, shared_prompt_keys)
    return (grad_rows[None], key_out, value_out)


def solution(mesh):
    in_specs = (
        P("comp", "prompt", None),
        P("comp", "prompt", None),
        P("comp", "prompt", None),
        P("comp", None, "prompt"),
        P("comp"),
        P("prompt", None),
        P("prompt", None),
    )
    out_specs = (P("comp", "prompt", None), P("prompt", None), P("prompt", None))
    return jax.shard_map(shards, mesh=mesh, in_specs=in_specs, out_specs=out_specs, check_vma=False)
```

```python
import jax
import jax.numpy as jnp
from jax import lax
from jax.experimental import pallas as pl
from jax.experimental.pallas import tpu as pltpu
from jax.sharding import PartitionSpec as P

HEAD_SIZE = 128
SCALE = 1.0 / HEAD_SIZE**0.5
LOG2_E = 1.4426950408889634
CORES = 2
SMALL_VMEM = 8 * 1024 * 1024
LARGE_VMEM = 24 * 1024 * 1024
FULL_VMEM = 56 * 1024 * 1024
PIECES = 4


def rows_by_rows(a, b):
    return lax.dot_general(a, b, (((1,), (1,)), ((), ())), preferred_element_type=jnp.float32)


def own_core():
    return lax.rem(lax.axis_index("comp"), CORES)


def spread_kernel(k_ref, v_ref, out_ref):
    half = k_ref.shape[1] // CORES
    at = pl.ds(pl.multiple_of(own_core() * half, half), half)
    both = jnp.concatenate([k_ref[:, at], v_ref[:, at]], axis=1)
    for i in range(out_ref.shape[0]):
        out_ref[i] = both


def spread(keys, values, owners):
    own, width = keys.shape
    return pl.pallas_call(
        spread_kernel,
        out_shape=jax.ShapeDtypeStruct((owners, own, 2 * width // CORES), keys.dtype),
        compiler_params=pltpu.CompilerParams(vmem_limit_bytes=FULL_VMEM),
        name="spread",
    )(keys, values)


def delta_kernel(live_ref, g_ref, o_ref, delta_ref, keep_ref):
    rows, wide = o_ref.shape
    heads = wide // HEAD_SIZE
    step = pl.program_id(0)
    live = lax.broadcasted_iota(jnp.int32, (rows, HEAD_SIZE), 0) < live_ref[0]
    keep_ref[...] = live.astype(jnp.float32)
    columns = []
    for h in range(heads):
        cut = slice(h * HEAD_SIZE, (h + 1) * HEAD_SIZE)
        at = pl.ds(pl.multiple_of(step * wide + h * HEAD_SIZE, HEAD_SIZE), HEAD_SIZE)
        product = g_ref[:, at].astype(jnp.float32) * o_ref[:, cut].astype(jnp.float32)
        columns.append(jnp.sum(jnp.where(live, product, 0.0), axis=1, keepdims=True))
    own = pl.ds(pl.multiple_of(step * heads, heads), heads)
    delta_ref[own, :] = jnp.concatenate(columns, axis=1).T


def row_delta(live, grad_out, outputs, heads, steps):
    rows, width = grad_out.shape
    vmem = pl.BlockSpec(memory_space=pltpu.VMEM)
    return pl.pallas_call(
        delta_kernel,
        grid=(steps,),
        in_specs=[
            pl.BlockSpec(memory_space=pltpu.SMEM),
            vmem,
            pl.BlockSpec((rows, width // steps), lambda h: (0, h)),
        ],
        out_specs=[vmem, vmem],
        out_shape=[
            jax.ShapeDtypeStruct((heads, rows), jnp.float32),
            jax.ShapeDtypeStruct((rows, HEAD_SIZE), jnp.float32),
        ],
        compiler_params=pltpu.CompilerParams(vmem_limit_bytes=SMALL_VMEM),
        cost_estimate=pl.CostEstimate(
            flops=3 * rows * width, bytes_accessed=4 * rows * width, transcendentals=0
        ),
        name="delta",
    )(live, grad_out, outputs)


def scores_and_dprobs(keys, values, q, g):
    return rows_by_rows(keys, q), rows_by_rows(values, g)


def probs_and_dscores(scores, dprobs, rest, delta):
    scale = LOG2_E * SCALE
    rest = rest * LOG2_E
    top = jnp.maximum(jnp.max(scores, axis=0, keepdims=True) * scale, rest)
    weights = jnp.exp2(scores * scale - top)
    total = jnp.sum(weights, axis=0, keepdims=True) + jnp.exp2(rest - top)
    probs = weights * (1.0 / total)
    dscores = probs * (dprobs - delta)
    return probs.astype(jnp.bfloat16), dscores.astype(jnp.bfloat16)


def side_by_side(tile):
    return jnp.concatenate([tile[h : h + 1] for h in range(tile.shape[0])], axis=1)


def place_half(side, half_ref, rows_hbm, sems):
    width = half_ref.shape[1]
    pieces = sems.shape[0]
    piece = width // pieces
    copies = []
    for i in range(pieces):
        to = pl.ds(pl.multiple_of(side * width + i * piece, piece), piece)
        copies.append(
            pltpu.make_async_copy(
                half_ref.at[:, i * piece : (i + 1) * piece], rows_hbm.at[:, to], sems.at[i]
            )
        )
        copies[-1].start()
    return copies


def query_gradients(keys, dscores, rows, dq_ref, at):
    dq = jnp.dot(keys.T, dscores, preferred_element_type=jnp.float32) * SCALE
    dq = dq.astype(dq_ref.dtype)
    for h in range(dq.shape[1] // rows):
        cut = slice(at + h * HEAD_SIZE, at + (h + 1) * HEAD_SIZE)
        dq_ref[:, cut] = dq[:, h * rows : (h + 1) * rows].T


def key_cuts(width, steps):
    return [
        tuple(
            slice(side * width // 2 + i * HEAD_SIZE, side * width // 2 + (i + 1) * HEAD_SIZE)
            for side in range(2)
        )
        for i in range(steps)
    ]


def softmax_backward(side, steps, kv_ref, q_ref, g_ref, rest_ref, delta_ref, keep_ref):
    rows = q_ref.shape[0]
    wide = q_ref.shape[1] // (CORES * steps)
    group = wide // HEAD_SIZE
    first = side * steps
    keep = keep_ref[...]
    held = []
    for i, (key_at, value_at) in enumerate(key_cuts(kv_ref.shape[1], steps)):
        at = pl.multiple_of((first + i) * wide, wide)
        columns = [pl.ds(at + h * HEAD_SIZE, HEAD_SIZE) for h in range(group)]
        q = jnp.concatenate([q_ref[:, cut] for cut in columns], axis=0)
        g = jnp.concatenate(
            [(g_ref[:, cut].astype(jnp.float32) * keep).astype(jnp.bfloat16) for cut in columns],
            axis=0,
        )
        held.append((q, g, *scores_and_dprobs(kv_ref[:, key_at], kv_ref[:, value_at], q, g)))
    for i, (q, g, scores, dprobs) in enumerate(held):
        own = pl.ds(pl.multiple_of((first + i) * group, group), group)
        yield q, g, *probs_and_dscores(
            scores, dprobs, side_by_side(rest_ref[own, :]), side_by_side(delta_ref[own, :])
        )


def near_kernel(
    q_ref, g_ref, rest_ref, delta_ref, keep_ref, kv_ref, packet_ref, dscores_ref
):
    prompt, width = kv_ref.shape
    steps = width // (2 * HEAD_SIZE)
    wide = dscores_ref.shape[1] // steps
    packet_ref[:prompt, :] = kv_ref[...]
    parts = softmax_backward(
        own_core(), steps, kv_ref, q_ref, g_ref, rest_ref, delta_ref, keep_ref
    )
    for i, (q, g, probs, dscores) in enumerate(parts):
        key_at, value_at = key_cuts(width, steps)[i]
        dscores_ref[:, i * wide : (i + 1) * wide] = dscores
        key_terms = jnp.dot(dscores, q, preferred_element_type=jnp.float32) * SCALE
        value_terms = jnp.dot(probs, g, preferred_element_type=jnp.float32)
        packet_ref[prompt:, key_at] = key_terms.astype(packet_ref.dtype)
        packet_ref[prompt:, value_at] = value_terms.astype(packet_ref.dtype)


def near_rows_kernel(dscores_ref, kv_ref, dq_ref):
    rows, width = dq_ref.shape
    steps = kv_ref.shape[1] // (2 * HEAD_SIZE)
    wide = width // steps
    for i, (key_at, _) in enumerate(key_cuts(kv_ref.shape[1], steps)):
        dscores = dscores_ref[:, i * wide : (i + 1) * wide]
        query_gradients(kv_ref[:, key_at], dscores, rows, dq_ref, i * wide)


def far_kernel(
    q_ref,
    g_ref,
    rest_ref,
    delta_ref,
    keep_ref,
    packet_ref,
    near_ref,
    dq_ref,
    terms_ref,
    rows_hbm,
    sems,
):
    copies = place_half(own_core(), near_ref, rows_hbm, sems)
    prompt, width = terms_ref.shape
    rows = dq_ref.shape[0]
    steps = width // (2 * HEAD_SIZE)
    wide = dq_ref.shape[1] // steps
    kv_ref = packet_ref.at[:prompt, :]
    parts = softmax_backward(
        1 - own_core(), steps, kv_ref, q_ref, g_ref, rest_ref, delta_ref, keep_ref
    )
    for i, (q, g, probs, dscores) in enumerate(parts):
        key_at, value_at = key_cuts(width, steps)[i]
        query_gradients(kv_ref[:, key_at], dscores, rows, dq_ref, i * wide)
        key_terms = jnp.dot(dscores, q, preferred_element_type=jnp.float32) * SCALE
        value_terms = jnp.dot(probs, g, preferred_element_type=jnp.float32)
        terms_ref[:, key_at] = key_terms
        terms_ref[:, value_at] = value_terms
    for copy in copies:
        copy.wait()


def call(kernel, name, flops, out_shape, *operands, in_float32=(), in_hbm=(), scratch=()):
    vmem = pl.BlockSpec(memory_space=pltpu.VMEM)
    hbm = pl.BlockSpec(memory_space=pltpu.HBM)
    return pl.pallas_call(
        kernel,
        in_specs=[vmem] * len(operands),
        out_specs=[hbm if i in in_hbm else vmem for i in range(len(out_shape))],
        out_shape=[
            jax.ShapeDtypeStruct(shape, jnp.float32 if i in in_float32 else jnp.bfloat16)
            for i, shape in enumerate(out_shape)
        ],
        scratch_shapes=list(scratch),
        compiler_params=pltpu.CompilerParams(vmem_limit_bytes=LARGE_VMEM),
        cost_estimate=pl.CostEstimate(flops=flops, bytes_accessed=2**20, transcendentals=0),
        name=name,
    )(*operands)


def place_half(side, half_ref, rows_hbm, sems):
    width = half_ref.shape[1]
    pieces = sems.shape[0]
    piece = width // pieces
    copies = []
    for i in range(pieces):
        to = pl.ds(pl.multiple_of(side * width + i * piece, piece), piece)
        copies.append(
            pltpu.make_async_copy(
                half_ref.at[:, i * piece : (i + 1) * piece], rows_hbm.at[:, to], sems.at[i]
            )
        )
        copies[-1].start()
    return copies


def finish_kernel(parts_ref, far_ref, before_hbm, key_ref, value_ref, rows_ref):
    turn = pl.program_id(0)
    first = CORES - 1 - turn
    total = parts_ref[first].astype(jnp.float32)
    for i in range(CORES, parts_ref.shape[0], CORES):
        total += parts_ref[first + i].astype(jnp.float32)
    half = total.shape[1] // 2
    key_ref[...] = total[:, :half].astype(key_ref.dtype)
    value_ref[...] = total[:, half:].astype(value_ref.dtype)
    width = rows_ref.shape[1]
    rows_ref[...] = far_ref[:, pl.ds(pl.multiple_of(turn * width, width), width)]


def finish(parts, far, grad_rows, like):
    vmem = pl.BlockSpec(memory_space=pltpu.VMEM)
    hbm = pl.BlockSpec(memory_space=pltpu.HBM)
    one = jax.ShapeDtypeStruct(like.shape, like.dtype)
    own, width = like.shape
    piece = (far.shape[0], far.shape[1] // CORES)
    return pl.pallas_call(
        finish_kernel,
        grid=(CORES,),
        in_specs=[vmem, vmem, hbm],
        out_specs=[
            pl.BlockSpec((own, width // CORES), lambda i: (0, i)),
            pl.BlockSpec((own, width // CORES), lambda i: (0, i)),
            pl.BlockSpec(piece, lambda i: (0, (1 - own_core()) * CORES + i)),
        ],
        out_shape=[one, one, jax.ShapeDtypeStruct(grad_rows.shape, grad_rows.dtype)],
        input_output_aliases={2: 2},
        compiler_params=pltpu.CompilerParams(vmem_limit_bytes=SMALL_VMEM),
        name="finish",
    )(parts, far, grad_rows)


def shards(
    queries,
    grad_out,
    outputs,
    completion_log_sum_exp,
    lengths,
    shared_prompt_keys,
    shared_prompt_values,
):
    rows = queries.shape[1]
    own, kv_width = shared_prompt_keys.shape
    heads = completion_log_sum_exp.shape[1]
    owners = lax.axis_size("prompt")
    members = lax.axis_size("comp")
    other_core = [(i, i ^ 1) for i in range(members)]
    live = lengths - lax.axis_index("prompt") * rows
    rest = completion_log_sum_exp[0]

    near = lax.all_to_all(
        spread(shared_prompt_keys, shared_prompt_values, owners), "prompt", 0, 0
    ).reshape(owners * own, kv_width)
    delta, keep = row_delta(live, grad_out[0], outputs[0], heads, kv_width // HEAD_SIZE)
    width = queries.shape[2]
    half = (rows, width // CORES)
    prompt = near.shape[0]
    product = rows * width // CORES * prompt * 2
    given = (queries[0], grad_out[0], rest, delta, keep)
    packet, dscores = call(
        near_kernel,
        "near",
        4 * product,
        [(2 * prompt, kv_width), (prompt, width // CORES)],
        *given,
        near,
    )
    received = lax.ppermute(packet, "comp", other_core)
    (grad_near,) = call(near_rows_kernel, "near_rows", product, [half], dscores, near)
    grad_far, kept, grad_rows = call(
        far_kernel,
        "far",
        5 * product,
        [half, near.shape, (rows, width)],
        *given,
        received,
        grad_near,
        in_float32=(1,),
        in_hbm=(2,),
        scratch=[pltpu.SemaphoreType.DMA((PIECES,))],
    )
    terms = (kept + received[prompt:].astype(jnp.float32)).astype(jnp.bfloat16)
    shares = lax.all_to_all(terms.reshape(owners, own, kv_width), "prompt", 0, 0)
    share = jnp.sum(shares.astype(jnp.float32), axis=0).astype(jnp.bfloat16)
    parts = lax.all_to_all(
        jnp.broadcast_to(share[None], (members, own, kv_width)), "comp", 0, 0
    )
    key_out, value_out, grad_rows = finish(parts, grad_far, grad_rows, shared_prompt_keys)
    return (grad_rows[None], key_out, value_out)


def solution(mesh):
    in_specs = (
        P("comp", "prompt", None),
        P("comp", "prompt", None),
        P("comp", "prompt", None),
        P("comp", None, "prompt"),
        P("comp"),
        P("prompt", None),
        P("prompt", None),
    )
    out_specs = (P("comp", "prompt", None), P("prompt", None), P("prompt", None))
    return jax.shard_map(shards, mesh=mesh, in_specs=in_specs, out_specs=out_specs, check_vma=False)
```

```python
import jax
import jax.numpy as jnp
from jax import lax
from jax.experimental import pallas as pl
from jax.experimental.pallas import tpu as pltpu
from jax.sharding import PartitionSpec as P

HEAD_SIZE = 128
SCALE = 1.0 / HEAD_SIZE**0.5
LOG2_E = 1.4426950408889634
CORES = 2
SMALL_VMEM = 8 * 1024 * 1024
LARGE_VMEM = 24 * 1024 * 1024
FULL_VMEM = 56 * 1024 * 1024
PIECES = 4


def rows_by_rows(a, b):
    return lax.dot_general(a, b, (((1,), (1,)), ((), ())), preferred_element_type=jnp.float32)


def own_core():
    return lax.rem(lax.axis_index("comp"), CORES)


def spread_kernel(k_ref, v_ref, out_ref):
    half = k_ref.shape[1] // CORES
    at = pl.ds(pl.multiple_of(own_core() * half, half), half)
    both = jnp.concatenate([k_ref[:, at], v_ref[:, at]], axis=1)
    for i in range(out_ref.shape[0]):
        out_ref[i] = both


def spread(keys, values, owners):
    own, width = keys.shape
    return pl.pallas_call(
        spread_kernel,
        out_shape=jax.ShapeDtypeStruct((owners, own, 2 * width // CORES), keys.dtype),
        compiler_params=pltpu.CompilerParams(vmem_limit_bytes=FULL_VMEM),
        name="spread",
    )(keys, values)


def delta_kernel(live_ref, g_ref, o_ref, delta_ref, masked_ref):
    rows, wide = o_ref.shape
    heads = wide // HEAD_SIZE
    step = pl.program_id(0)
    keep = lax.broadcasted_iota(jnp.int32, (rows, HEAD_SIZE), 0) < live_ref[0]
    keep = keep.astype(jnp.float32)
    columns = []
    for h in range(heads):
        cut = slice(h * HEAD_SIZE, (h + 1) * HEAD_SIZE)
        at = pl.ds(pl.multiple_of(step * wide + h * HEAD_SIZE, HEAD_SIZE), HEAD_SIZE)
        masked = g_ref[:, cut].astype(jnp.float32) * keep
        masked_ref[:, at] = masked.astype(masked_ref.dtype)
        product = masked * o_ref[:, cut].astype(jnp.float32)
        columns.append(jnp.sum(product, axis=1, keepdims=True))
    own = pl.ds(pl.multiple_of(step * heads, heads), heads)
    delta_ref[own, :] = jnp.concatenate(columns, axis=1).T


def row_delta(live, grad_out, outputs, heads, steps):
    rows, width = grad_out.shape
    vmem = pl.BlockSpec(memory_space=pltpu.VMEM)
    return pl.pallas_call(
        delta_kernel,
        grid=(steps,),
        in_specs=[
            pl.BlockSpec(memory_space=pltpu.SMEM),
            pl.BlockSpec((rows, width // steps), lambda h: (0, h)),
            pl.BlockSpec((rows, width // steps), lambda h: (0, h)),
        ],
        out_specs=[vmem, vmem],
        out_shape=[
            jax.ShapeDtypeStruct((heads, rows), jnp.float32),
            jax.ShapeDtypeStruct((rows, width), grad_out.dtype),
        ],
        compiler_params=pltpu.CompilerParams(vmem_limit_bytes=SMALL_VMEM),
        cost_estimate=pl.CostEstimate(
            flops=3 * rows * width, bytes_accessed=4 * rows * width, transcendentals=0
        ),
        name="delta",
    )(live, grad_out, outputs)


def scores_and_dprobs(keys, values, q, g):
    return rows_by_rows(keys, q), rows_by_rows(values, g)


def probs_and_dscores(scores, dprobs, rest, delta):
    scale = LOG2_E * SCALE
    rest = rest * LOG2_E
    top = jnp.maximum(jnp.max(scores, axis=0, keepdims=True) * scale, rest)
    weights = jnp.exp2(scores * scale - top)
    total = jnp.sum(weights, axis=0, keepdims=True) + jnp.exp2(rest - top)
    probs = weights * (1.0 / total)
    dscores = probs * (dprobs - delta)
    return probs.astype(jnp.bfloat16), dscores.astype(jnp.bfloat16)


def side_by_side(tile):
    return jnp.concatenate([tile[h : h + 1] for h in range(tile.shape[0])], axis=1)


def place_half(side, half_ref, rows_hbm, sems):
    width = half_ref.shape[1]
    pieces = sems.shape[0]
    piece = width // pieces
    copies = []
    for i in range(pieces):
        to = pl.ds(pl.multiple_of(side * width + i * piece, piece), piece)
        copies.append(
            pltpu.make_async_copy(
                half_ref.at[:, i * piece : (i + 1) * piece], rows_hbm.at[:, to], sems.at[i]
            )
        )
        copies[-1].start()
    return copies


def query_gradients(keys, dscores, rows, dq_ref, at):
    dq = jnp.dot(keys.T, dscores, preferred_element_type=jnp.float32) * SCALE
    dq = dq.astype(dq_ref.dtype)
    for h in range(dq.shape[1] // rows):
        cut = slice(at + h * HEAD_SIZE, at + (h + 1) * HEAD_SIZE)
        dq_ref[:, cut] = dq[:, h * rows : (h + 1) * rows].T


def key_cuts(width, steps):
    return [
        tuple(
            slice(side * width // 2 + i * HEAD_SIZE, side * width // 2 + (i + 1) * HEAD_SIZE)
            for side in range(2)
        )
        for i in range(steps)
    ]


def softmax_backward(side, steps, kv_ref, q_ref, g_ref, rest_ref, delta_ref):
    rows = q_ref.shape[0]
    wide = q_ref.shape[1] // (CORES * steps)
    group = wide // HEAD_SIZE
    first = side * steps
    held = []
    for i, (key_at, value_at) in enumerate(key_cuts(kv_ref.shape[1], steps)):
        at = pl.multiple_of((first + i) * wide, wide)
        columns = [pl.ds(at + h * HEAD_SIZE, HEAD_SIZE) for h in range(group)]
        q = jnp.concatenate([q_ref[:, cut] for cut in columns], axis=0)
        g = jnp.concatenate([g_ref[:, cut] for cut in columns], axis=0)
        held.append((q, g, *scores_and_dprobs(kv_ref[:, key_at], kv_ref[:, value_at], q, g)))
    for i, (q, g, scores, dprobs) in enumerate(held):
        own = pl.ds(pl.multiple_of((first + i) * group, group), group)
        yield q, g, *probs_and_dscores(
            scores, dprobs, side_by_side(rest_ref[own, :]), side_by_side(delta_ref[own, :])
        )


def near_kernel(
    q_ref, g_ref, rest_ref, delta_ref, kv_ref, packet_ref, dscores_ref
):
    prompt, width = kv_ref.shape
    steps = width // (2 * HEAD_SIZE)
    wide = dscores_ref.shape[1] // steps
    packet_ref[:prompt, :] = kv_ref[...]
    parts = softmax_backward(
        own_core(), steps, kv_ref, q_ref, g_ref, rest_ref, delta_ref
    )
    for i, (q, g, probs, dscores) in enumerate(parts):
        key_at, value_at = key_cuts(width, steps)[i]
        dscores_ref[:, i * wide : (i + 1) * wide] = dscores
        key_terms = jnp.dot(dscores, q, preferred_element_type=jnp.float32) * SCALE
        value_terms = jnp.dot(probs, g, preferred_element_type=jnp.float32)
        packet_ref[prompt:, key_at] = key_terms.astype(packet_ref.dtype)
        packet_ref[prompt:, value_at] = value_terms.astype(packet_ref.dtype)


def near_rows_kernel(dscores_ref, kv_ref, dq_ref):
    rows, width = dq_ref.shape
    steps = kv_ref.shape[1] // (2 * HEAD_SIZE)
    wide = width // steps
    for i, (key_at, _) in enumerate(key_cuts(kv_ref.shape[1], steps)):
        dscores = dscores_ref[:, i * wide : (i + 1) * wide]
        query_gradients(kv_ref[:, key_at], dscores, rows, dq_ref, i * wide)


def far_kernel(
    q_ref,
    g_ref,
    rest_ref,
    delta_ref,
    packet_ref,
    near_ref,
    dq_ref,
    terms_ref,
    rows_hbm,
    sems,
):
    copies = place_half(own_core(), near_ref, rows_hbm, sems)
    prompt, width = terms_ref.shape
    rows = dq_ref.shape[0]
    steps = width // (2 * HEAD_SIZE)
    wide = dq_ref.shape[1] // steps
    kv_ref = packet_ref.at[:prompt, :]
    parts = softmax_backward(
        1 - own_core(), steps, kv_ref, q_ref, g_ref, rest_ref, delta_ref
    )
    for i, (q, g, probs, dscores) in enumerate(parts):
        key_at, value_at = key_cuts(width, steps)[i]
        query_gradients(kv_ref[:, key_at], dscores, rows, dq_ref, i * wide)
        key_terms = jnp.dot(dscores, q, preferred_element_type=jnp.float32) * SCALE
        value_terms = jnp.dot(probs, g, preferred_element_type=jnp.float32)
        terms_ref[:, key_at] = key_terms
        terms_ref[:, value_at] = value_terms
    for copy in copies:
        copy.wait()


def call(kernel, name, flops, out_shape, *operands, in_float32=(), in_hbm=(), scratch=()):
    vmem = pl.BlockSpec(memory_space=pltpu.VMEM)
    hbm = pl.BlockSpec(memory_space=pltpu.HBM)
    return pl.pallas_call(
        kernel,
        in_specs=[vmem] * len(operands),
        out_specs=[hbm if i in in_hbm else vmem for i in range(len(out_shape))],
        out_shape=[
            jax.ShapeDtypeStruct(shape, jnp.float32 if i in in_float32 else jnp.bfloat16)
            for i, shape in enumerate(out_shape)
        ],
        scratch_shapes=list(scratch),
        compiler_params=pltpu.CompilerParams(vmem_limit_bytes=LARGE_VMEM),
        cost_estimate=pl.CostEstimate(flops=flops, bytes_accessed=2**20, transcendentals=0),
        name=name,
    )(*operands)


def place_half(side, half_ref, rows_hbm, sems):
    width = half_ref.shape[1]
    pieces = sems.shape[0]
    piece = width // pieces
    copies = []
    for i in range(pieces):
        to = pl.ds(pl.multiple_of(side * width + i * piece, piece), piece)
        copies.append(
            pltpu.make_async_copy(
                half_ref.at[:, i * piece : (i + 1) * piece], rows_hbm.at[:, to], sems.at[i]
            )
        )
        copies[-1].start()
    return copies


def finish_kernel(parts_ref, far_ref, before_hbm, key_ref, value_ref, rows_ref):
    turn = pl.program_id(0)
    first = CORES - 1 - turn
    total = parts_ref[first].astype(jnp.float32)
    for i in range(CORES, parts_ref.shape[0], CORES):
        total += parts_ref[first + i].astype(jnp.float32)
    half = total.shape[1] // 2
    key_ref[...] = total[:, :half].astype(key_ref.dtype)
    value_ref[...] = total[:, half:].astype(value_ref.dtype)
    width = rows_ref.shape[1]
    rows_ref[...] = far_ref[:, pl.ds(pl.multiple_of(turn * width, width), width)]


def finish(parts, far, grad_rows, like):
    vmem = pl.BlockSpec(memory_space=pltpu.VMEM)
    hbm = pl.BlockSpec(memory_space=pltpu.HBM)
    one = jax.ShapeDtypeStruct(like.shape, like.dtype)
    own, width = like.shape
    piece = (far.shape[0], far.shape[1] // CORES)
    return pl.pallas_call(
        finish_kernel,
        grid=(CORES,),
        in_specs=[vmem, vmem, hbm],
        out_specs=[
            pl.BlockSpec((own, width // CORES), lambda i: (0, i)),
            pl.BlockSpec((own, width // CORES), lambda i: (0, i)),
            pl.BlockSpec(piece, lambda i: (0, (1 - own_core()) * CORES + i)),
        ],
        out_shape=[one, one, jax.ShapeDtypeStruct(grad_rows.shape, grad_rows.dtype)],
        input_output_aliases={2: 2},
        compiler_params=pltpu.CompilerParams(vmem_limit_bytes=SMALL_VMEM),
        name="finish",
    )(parts, far, grad_rows)


def shards(
    queries,
    grad_out,
    outputs,
    completion_log_sum_exp,
    lengths,
    shared_prompt_keys,
    shared_prompt_values,
):
    rows = queries.shape[1]
    own, kv_width = shared_prompt_keys.shape
    heads = completion_log_sum_exp.shape[1]
    owners = lax.axis_size("prompt")
    members = lax.axis_size("comp")
    other_core = [(i, i ^ 1) for i in range(members)]
    live = lengths - lax.axis_index("prompt") * rows
    rest = completion_log_sum_exp[0]

    near = lax.all_to_all(
        spread(shared_prompt_keys, shared_prompt_values, owners), "prompt", 0, 0
    ).reshape(owners * own, kv_width)
    delta, masked = row_delta(live, grad_out[0], outputs[0], heads, kv_width // HEAD_SIZE)
    width = queries.shape[2]
    half = (rows, width // CORES)
    prompt = near.shape[0]
    product = rows * width // CORES * prompt * 2
    given = (queries[0], masked, rest, delta)
    packet, dscores = call(
        near_kernel,
        "near",
        4 * product,
        [(2 * prompt, kv_width), (prompt, width // CORES)],
        *given,
        near,
    )
    received = lax.ppermute(packet, "comp", other_core)
    (grad_near,) = call(near_rows_kernel, "near_rows", product, [half], dscores, near)
    grad_far, kept, grad_rows = call(
        far_kernel,
        "far",
        5 * product,
        [half, near.shape, (rows, width)],
        *given,
        received,
        grad_near,
        in_float32=(1,),
        in_hbm=(2,),
        scratch=[pltpu.SemaphoreType.DMA((PIECES,))],
    )
    terms = (kept + received[prompt:].astype(jnp.float32)).astype(jnp.bfloat16)
    shares = lax.all_to_all(terms.reshape(owners, own, kv_width), "prompt", 0, 0)
    share = jnp.sum(shares.astype(jnp.float32), axis=0).astype(jnp.bfloat16)
    parts = lax.all_to_all(
        jnp.broadcast_to(share[None], (members, own, kv_width)), "comp", 0, 0
    )
    key_out, value_out, grad_rows = finish(parts, grad_far, grad_rows, shared_prompt_keys)
    return (grad_rows[None], key_out, value_out)


def solution(mesh):
    in_specs = (
        P("comp", "prompt", None),
        P("comp", "prompt", None),
        P("comp", "prompt", None),
        P("comp", None, "prompt"),
        P("comp"),
        P("prompt", None),
        P("prompt", None),
    )
    out_specs = (P("comp", "prompt", None), P("prompt", None), P("prompt", None))
    return jax.shard_map(shards, mesh=mesh, in_specs=in_specs, out_specs=out_specs, check_vma=False)
```
